32 devices in a mesh: ctx: 8 (over z, x), tp: 4 (over y, core).
Axes of the slice: x: 2, y: 2, z: 4, core: 2. Of those that a mesh axis runs over, the one named last changes fastest.
Arguments:
- ssm_input: bfloat16 [4096, 16384], P('ctx', 'tp'), may hold values from -6 to 6
- gate_input: bfloat16 [4096, 16384], P('ctx', 'tp'), may hold values from -6 to 6
- state_maps: bfloat16 [4096, 2, 1024], P('ctx', None, 'tp'), may hold values from -6 to 6
- step_size: float32 [4096, 256], P('ctx', 'tp'), may hold values from 0 to 8, as said below
- decay_rate: float32 [256], P('tp'), may hold values from 0 to 1, as said below
- skip_gain: float32 [256], P('tp'), may hold values from 0.5 to 1.5
- conv_weight: float32 [4, 16384], P(None, 'tp'), may hold values from -0.5 to 0.5
- conv_bias: float32 [16384], P('tp'), may hold values from -0.5 to 0.5
- map_conv: float32 [4, 2, 1024], P(None, None, 'tp'), may hold values from -0.5 to 0.5
- map_bias: float32 [2, 1024], P(None, 'tp'), may hold values from -1 to 1
- norm_gain: float32 [16384], P('tp'), may hold values from 0.1 to 1.9
- out_weight: bfloat16 [16384, 4096], P('tp'), may hold values from -0.046875 to 0.046875
Outputs:
- mixer_out: bfloat16 [4096, 4096], P(('ctx', 'tp'))
The draws below stay inside these ranges and needn't reach their ends.
Inputs may be any that keep to these rules, and one draw needn't show every extreme that they name: `step_size`: positive step of every token and head. `decay_rate`: positive rate of every head.
All inputs are finite; a program needn't handle non-finite values.
Results may differ from the reference program's by a relative error of at most 0.03.
Values may be sent and summed in bfloat16 or wider, within the bound.
A program may use at most 192 MiB of HBM per device.

```python
import math
import jax
import jax.numpy as jnp
from jax import lax

MIXER_HEADS = 256
HEAD_DIM = 64
STATE = 128
GROUPS = 8
CONV = 4
BLOCK = 128
D_OUT = 4096
TOK_DEV = 512
D_INNER = 16384
SEQUENCE_TOKENS = 4096
N_TP = 4


def decay_tables(key):
    base_key = jax.random.fold_in(key, 4099)
    random_keys = jax.random.split(base_key, 8)
    slow_share = 0.5
    slow_flag = jax.random.uniform(random_keys[1], (MIXER_HEADS,), jnp.float32) < slow_share
    slow_total = jnp.exp(jax.random.uniform(random_keys[2], (MIXER_HEADS,), jnp.float32, math.log(0.05), math.log(0.3)))
    slow_rate = slow_total / SEQUENCE_TOKENS
    fast_reach = jnp.exp(jax.random.uniform(random_keys[3], (MIXER_HEADS,), jnp.float32, math.log(30.0), math.log(50.0)))
    per_token = jnp.where(slow_flag, slow_rate, 1.0 / fast_reach)
    head_rate = per_token / 0.5
    block_factor = jnp.exp(jax.random.uniform(random_keys[4], (SEQUENCE_TOKENS // TOK_DEV,), jnp.float32, math.log(0.6), math.log(1.5)))
    block_factor = jnp.repeat(block_factor, TOK_DEV)
    roughness = jax.random.uniform(random_keys[5], (SEQUENCE_TOKENS, MIXER_HEADS), jnp.float32, 0.5, 1.5)
    steps = 0.5 * block_factor[:, None] * roughness
    spike_rows = jax.random.randint(random_keys[6], (2,), 0, SEQUENCE_TOKENS)
    spike_loss = jax.random.uniform(random_keys[7], (2, MIXER_HEADS), jnp.float32, 0.22, 0.69)
    spike_steps = jnp.minimum(spike_loss / head_rate[None, :], 8.0)
    token_places = jnp.arange(SEQUENCE_TOKENS)
    steps = jnp.where((token_places == spike_rows[0])[:, None], spike_steps[0][None, :], steps)
    steps = jnp.where((token_places == spike_rows[1])[:, None], spike_steps[1][None, :], steps)
    return (head_rate, steps)


def draw_decay_rate(key, part):
    return decay_tables(key)[0]


def draw_step_size(key, part):
    return decay_tables(key)[1]


def level_of(key, extent, shards, smallest, high):
    def one(position, parts):
        heights = jax.random.uniform(jax.random.fold_in(jax.random.fold_in(key, 6), position), (parts,), jnp.float32, smallest / len(shards), high / len(shards))
        return jnp.repeat(jnp.exp(heights), extent[position] // parts).reshape((-1,) + (1,) * (len(extent) - position - 1))

    loudness = one(*shards[0])
    for cut in shards[1:]:
        loudness = loudness * one(*cut)
    return loudness


def gaussian(own_key, extent, scale, most, cuts=(), kind=jnp.bfloat16):
    result = scale * jax.random.normal(own_key, extent, jnp.float32)
    if cuts:
        result = result * level_of(own_key, extent, cuts, -0.22, 0.18)
    return jnp.clip(result, -most, most).astype(kind)


def setup_inputs(seed: int = 0) -> dict:
    splits = jax.random.split(jax.random.key(seed), 13)
    ssm_input = gaussian(splits[0], (SEQUENCE_TOKENS, D_INNER), 1.0, 6.0, ((0, 8), (1, 4)))
    gate_input = gaussian(splits[1], (SEQUENCE_TOKENS, D_INNER), 1.0, 6.0, ((0, 8), (1, 4)))
    state_maps = gaussian(splits[2], (SEQUENCE_TOKENS, 2, GROUPS * STATE), 1.0, 6.0, ((0, 8), (2, 4)))
    step_size = draw_step_size(jax.random.fold_in(splits[12], 71), 0)
    decay_rate = draw_decay_rate(jax.random.fold_in(splits[12], 71), 0)
    skip_gain = jnp.clip(0.5 + 1.0 * jax.random.uniform(splits[5], (MIXER_HEADS,), jnp.float32) ** level_of(splits[5], (MIXER_HEADS,), ((0, 4),), -0.2, 0.2), 0.5, 1.5)
    conv_weight = jnp.clip(jax.random.uniform(splits[6], (CONV, D_INNER), jnp.float32, -0.5, 0.5) * level_of(splits[6], (CONV, D_INNER), ((1, 4),), -0.4, 0.0), -0.5, 0.5)
    conv_bias = jnp.clip(jax.random.uniform(splits[7], (D_INNER,), jnp.float32, -0.5, 0.5) * level_of(splits[7], (D_INNER,), ((0, 4),), -0.4, 0.0), -0.5, 0.5)
    map_conv = jnp.clip(jax.random.uniform(splits[8], (CONV, 2, GROUPS * STATE), jnp.float32, -0.5, 0.5) * level_of(splits[8], (CONV, 2, GROUPS * STATE), ((2, 4),), -0.4, 0.0), -0.5, 0.5)
    map_bias = jnp.clip(jax.random.uniform(splits[9], (2, GROUPS * STATE), jnp.float32, -1.0, 1.0) * level_of(splits[9], (2, GROUPS * STATE), ((1, 4),), -0.4, 0.0), -1.0, 1.0)
    norm_gain = jnp.clip(1.0 + 0.18 * jax.random.normal(splits[10], (D_INNER,), jnp.float32), 0.1, 1.9)
    out_weight = gaussian(splits[11], (D_INNER, D_OUT), D_INNER ** -0.5, 0.046875, ((0, 4),))
    return {"ssm_input": ssm_input, "gate_input": gate_input, "state_maps": state_maps, "step_size": step_size, "decay_rate": decay_rate, "skip_gain": skip_gain, "conv_weight": conv_weight, "conv_bias": conv_bias, "map_conv": map_conv, "map_bias": map_bias, "norm_gain": norm_gain, "out_weight": out_weight}


def rounded(values):
    return lax.optimization_barrier(values.astype(jnp.bfloat16))

def causal_conv(values, weight, bias_term):
    lead_rows = jnp.zeros((CONV - 1,) + values.shape[1:], values.dtype)
    padded = jnp.concatenate([lead_rows, values], axis=0)
    length = values.shape[0]
    accum = jnp.zeros(values.shape, jnp.float32) + bias_term.astype(jnp.float32)
    for offset in range(CONV):
        accum = accum + weight[offset].astype(jnp.float32) * padded[offset:offset + length].astype(jnp.float32)
    return rounded(jax.nn.silu(accum))

def reference(ssm_input, gate_input, state_maps, step_size, decay_rate, skip_gain, conv_weight, conv_bias, map_conv, map_bias, norm_gain, out_weight):
    conv_out = causal_conv(ssm_input, conv_weight, conv_bias)
    maps_out = causal_conv(state_maps, map_conv, map_bias)
    repeat = MIXER_HEADS // GROUPS
    blocks = SEQUENCE_TOKENS // BLOCK
    inner_width = MIXER_HEADS * HEAD_DIM
    log_decay = -decay_rate[None, :] * step_size
    values = conv_out.reshape(blocks, BLOCK, MIXER_HEADS, HEAD_DIM)
    input_maps = maps_out[:, 0].reshape(blocks, BLOCK, GROUPS, STATE)
    output_maps = maps_out[:, 1].reshape(blocks, BLOCK, GROUPS, STATE)
    block_logs = log_decay.reshape(blocks, BLOCK, MIXER_HEADS)
    block_steps = step_size.reshape(blocks, BLOCK, MIXER_HEADS)
    gate_blocks = gate_input.reshape(blocks, BLOCK, inner_width)
    causal_mask = jnp.tril(jnp.ones((BLOCK, BLOCK), dtype=bool))

    def block_step(carry_state, inputs):
        block_values, input_map, output_map, log_block, step_block, gate_block = inputs
        running = jnp.cumsum(log_block, axis=0)
        scores = jnp.einsum('qgn,sgn->gqs', output_map.astype(jnp.float32), input_map.astype(jnp.float32))
        scores = jnp.repeat(scores, repeat, axis=0)
        head_major = running.T
        gap_log = head_major[:, :, None] - head_major[:, None, :]
        decays = jnp.exp(jnp.where(causal_mask[None], gap_log, -1e+30))
        weights = rounded(scores * decays * step_block.T[:, None, :])
        within = jnp.einsum('hqs,shp->qhp', weights.astype(jnp.float32), block_values.astype(jnp.float32))
        to_end = jnp.exp(running[-1][None, :] - running) * step_block
        input_heads = jnp.repeat(input_map, repeat, axis=1)
        loaded = rounded(input_heads.astype(jnp.float32) * to_end[:, :, None])
        fresh_state = jnp.einsum('shn,shp->hnp', loaded.astype(jnp.float32), block_values.astype(jnp.float32))
        carried = rounded(carry_state)
        output_heads = jnp.repeat(output_map, repeat, axis=1)
        before = jnp.exp(running)[:, :, None] * jnp.einsum('qhn,hnp->qhp', output_heads.astype(jnp.float32), carried.astype(jnp.float32))
        output = within + before + skip_gain[None, :, None] * block_values.astype(jnp.float32)
        gated = output.reshape(BLOCK, inner_width) * jax.nn.silu(gate_block.astype(jnp.float32))
        grouped = gated.reshape(BLOCK, GROUPS, inner_width // GROUPS)
        inverse_rms = lax.rsqrt(lax.optimization_barrier(jnp.mean(grouped * grouped, axis=2, keepdims=True)) + 1e-05)
        normed = (grouped * inverse_rms).reshape(BLOCK, inner_width) * norm_gain[None, :]
        new_state = jnp.exp(running[-1])[:, None, None] * carry_state + fresh_state
        return (new_state, normed.astype(jnp.bfloat16))
    initial = jnp.zeros((MIXER_HEADS, STATE, HEAD_DIM), jnp.float32)
    final_state, normed = lax.scan(block_step, initial, (values, input_maps, output_maps, block_logs, block_steps, gate_blocks))
    normed = normed.reshape(SEQUENCE_TOKENS, inner_width)
    share_width = inner_width // N_TP
    summed = jnp.zeros((SEQUENCE_TOKENS, D_OUT), jnp.float32)
    for block_index in range(N_TP):
        lower = block_index * share_width
        partial_sum = jnp.dot(normed[:, lower:lower + share_width].astype(jnp.float32), out_weight[lower:lower + share_width].astype(jnp.float32), preferred_element_type=jnp.float32)
        summed = summed + rounded(partial_sum).astype(jnp.float32)
    return summed.astype(jnp.bfloat16)
```

```python
import functools

import jax
import jax.numpy as jnp
from jax import lax
from jax.experimental import pallas as pl
from jax.experimental.pallas import tpu as pltpu
from jax.sharding import PartitionSpec as P

HEAD_DIM = 64
STATE = 128
CONV = 4
BLOCK = 128
WIDE = 512
LEAD = 8
HEADS = 64
F32 = jnp.float32
BF16 = jnp.bfloat16
MESH = pl.DeviceIdType.MESH


def silu(v):
    return v / (1.0 + jnp.exp(-v))


def dot(a, b):
    return jnp.dot(a, b, preferred_element_type=F32)


def two_parts(v):
    high = v.astype(BF16)
    low = (v - high.astype(F32)).astype(BF16)
    return jnp.concatenate([high, low], axis=1)


def spread_matrix(chunk, heads):
    rows = lax.broadcasted_iota(jnp.int32, (2 * heads, WIDE), 0)
    cols = lax.broadcasted_iota(jnp.int32, (2 * heads, WIDE), 1)
    rows = jnp.where(rows >= heads, rows - heads, rows)
    return jnp.where(rows == chunk * (WIDE // HEAD_DIM) + cols // HEAD_DIM, 1.0, 0.0).astype(BF16)


def conv_rows(padded, base, count, weight, bias):
    window = padded[pl.ds(base, count + LEAD), :]
    total = bias
    for tap in range(CONV):
        start = LEAD - CONV + 1 + tap
        total = total + weight[tap : tap + 1] * window[start : start + count]
    return silu(total)


def state_kernel(
    x_ref, lead_ref, cw_ref, cb_ref, maps_ref, mlead_ref, mw_ref, mb_ref, step_ref, rate_ref,
    xc_ref, mc_ref, bt_ref, rs_ref, s_ref, enter_ref, padded, mpadded, load, tot,
):
    chunk = pl.program_id(0)
    length = x_ref.shape[0]
    heads = step_ref.shape[1]
    blocks = length // BLOCK
    groups = bt_ref.shape[0]
    per_group = pl.num_programs(0) // groups
    half = 64

    @pl.when(chunk == 0)
    def _():
        mpadded[0:LEAD] = mlead_ref[...].astype(F32)
        mpadded[LEAD:] = maps_ref[...].astype(F32)
        for r in range(length // half):
            mapped = conv_rows(mpadded, r * half, half, mw_ref[...], mb_ref[...])
            mc_ref[r * half : (r + 1) * half] = mapped.astype(BF16)
        tri = (
            lax.broadcasted_iota(jnp.int32, (BLOCK, BLOCK), 0)
            >= lax.broadcasted_iota(jnp.int32, (BLOCK, BLOCK), 1)
        ).astype(F32)
        for b in range(blocks):
            rows = slice(b * BLOCK, (b + 1) * BLOCK)
            for g in range(groups):
                own = mc_ref[rows, g * STATE : (g + 1) * STATE].astype(F32)
                bt_ref[g, :, rows] = own.T.astype(BF16)
            step = step_ref[rows]
            running = jnp.dot(
                tri, -rate_ref[...] * step,
                precision=lax.Precision.HIGHEST, preferred_element_type=F32,
            )
            rs_ref[rows] = jnp.concatenate([running, step], axis=1)
            last = running[BLOCK - 1 : BLOCK]
            load[rows] = two_parts(jnp.exp(last - running) * step)
            tot[b] = jnp.broadcast_to(two_parts(jnp.exp(last)).astype(F32), (8, 2 * heads))

    spread = spread_matrix(chunk, heads)
    padded[0:LEAD] = lead_ref[...].astype(F32)

    def widen(r, _):
        at = pl.multiple_of(r * half, half)
        padded[pl.ds(at + LEAD, half), :] = x_ref[pl.ds(at, half), :].astype(F32)
        return 0

    lax.fori_loop(0, length // half, widen, 0)
    weight, bias = cw_ref[...], cb_ref[...]

    def conv(r, _):
        at = pl.multiple_of(r * half, half)
        xc_ref[pl.ds(at, half), :] = conv_rows(padded, at, half, weight, bias).astype(BF16)
        return 0

    lax.fori_loop(0, length // half, conv, 0)
    group = chunk // per_group
    state = jnp.zeros((STATE, WIDE), F32)
    for b in range(blocks):
        rows = slice(b * BLOCK, (b + 1) * BLOCK)
        if b > 0:
            enter_ref[b - 1, 0] = state.astype(BF16)
        scaled = (xc_ref[rows].astype(F32) * dot(load[rows], spread)).astype(BF16)
        fresh = dot(bt_ref[group, :, rows], scaled)
        if b > 0:
            keep = dot(tot[b].astype(BF16), spread)[0:1]
            state = keep * state + fresh
        else:
            state = fresh
    s_ref[0] = state.astype(BF16)


def within_kernel(
    pairs, xc_ref, mc_ref, bt_ref, rs_ref, skip_ref, s_ref, y_ref, inc_ref,
    rolled, flipped, scores, mine, theirs, got, chain_in, chain_out, back_out, back_in,
    log_send, log_recv, x_send, x_recv, c_send, c_recv, b_send, b_recv,
):
    i = pl.program_id(0)
    steps = pl.num_programs(0)
    length = rs_ref.shape[0]
    heads = rs_ref.shape[1] // 2
    blocks = length // BLOCK
    groups = bt_ref.shape[0]
    chunks = s_ref.shape[0]
    per_half = chunks // 2
    per_group = chunks // groups
    place = lax.axis_index("ctx")
    pair, side = place // 2, place % 2
    peer = {"ctx": pair * 2 + 1 - side}
    ahead = {"ctx": place + 2}
    behind = {"ctx": place - 2}

    def log_copy():
        return pltpu.make_async_remote_copy(
            mine, theirs, log_send, log_recv, device_id=peer, device_id_type=MESH
        )

    def x_copy(c):
        return pltpu.make_async_remote_copy(
            s_ref.at[(1 - side) * per_half + c], got.at[c], x_send.at[c], x_recv.at[c],
            device_id=peer, device_id_type=MESH,
        )

    def c_copy(c):
        return pltpu.make_async_remote_copy(
            chain_out.at[c], chain_in.at[c], c_send.at[c], c_recv.at[c],
            device_id=ahead, device_id_type=MESH,
        )

    def b_copy(c):
        return pltpu.make_async_remote_copy(
            back_out.at[c], back_in.at[c], b_send.at[c], b_recv.at[c],
            device_id=peer, device_id_type=MESH,
        )

    @pl.when(i == 0)
    def _():
        barrier = pltpu.get_barrier_semaphore()
        pl.semaphore_signal(barrier, inc=1, device_id=peer, device_id_type=MESH)

        @pl.when(pair > 0)
        def _():
            pl.semaphore_signal(barrier, inc=1, device_id=behind, device_id_type=MESH)

        @pl.when(pair < pairs - 1)
        def _():
            pl.semaphore_signal(barrier, inc=1, device_id=ahead, device_id_type=MESH)

        total = jnp.zeros((1, heads), F32)
        for b in range(blocks):
            total = total + rs_ref[(b + 1) * BLOCK - 1 : (b + 1) * BLOCK, 0:heads]
        keep = jnp.exp(total)
        mine[...] = jnp.broadcast_to(jnp.concatenate([keep, keep], axis=1), (8, 2 * heads))
        near = jnp.where(pair > 0, 1, 0) + jnp.where(pair < pairs - 1, 1, 0) + 1
        pl.semaphore_wait(barrier, near)
        log_copy().start()
        for c in range(per_half):
            x_copy(c).start()

    c = i - 1 - 2 * pair

    @pl.when(i == 1)
    def _():
        log_copy().wait_recv()

    @pl.when((c >= 0) & (c < per_half))
    def _():
        x_copy(c).wait_recv()

        @pl.when(pair > 0)
        def _():
            c_copy(c).wait_recv()

        spread = spread_matrix(side * per_half + c, heads)
        keep_mine = dot(two_parts(mine[:, 0:heads]), spread)[0:1]
        keep_theirs = dot(two_parts(theirs[:, 0:heads]), spread)[0:1]
        own = s_ref[side * per_half + c].astype(F32)
        other = got[c].astype(F32)
        early = side == 0
        first = jnp.where(early, own, other)
        second = jnp.where(early, other, own)
        keep_first = jnp.where(early, keep_mine, keep_theirs)
        keep_second = jnp.where(early, keep_theirs, keep_mine)
        before = jnp.where(pair > 0, chain_in[c].astype(F32), 0.0)
        middle = keep_first * before + first
        after = keep_second * middle + second
        back_out[c] = jnp.where(early, middle, before).astype(BF16)
        b_copy(c).start()

        @pl.when(pair < pairs - 1)
        def _():
            chain_out[c] = after.astype(BF16)
            c_copy(c).start()

        inc_ref[side * per_half + c] = jnp.where(early, before, middle).astype(BF16)

    @pl.when(i < chunks)
    def _():
        wide = pltpu.roll(rs_ref[...], (2 * heads - i * (WIDE // HEAD_DIM)) % (2 * heads), 1)
        rolled[...] = wide
        flipped[...] = wide.T
        group = i // per_group

        def block(b, _):
            at = pl.multiple_of(b * BLOCK, BLOCK)
            rows = pl.ds(at, BLOCK)
            out_map = mc_ref[rows, pl.ds(pl.multiple_of((groups + group) * STATE, STATE), STATE)]
            score = dot(out_map, bt_ref[group, :, rows])
            causal = (
                lax.broadcasted_iota(jnp.int32, (BLOCK, BLOCK), 0)
                >= lax.broadcasted_iota(jnp.int32, (BLOCK, BLOCK), 1)
            )
            lower = lax.broadcasted_iota(jnp.int32, (BLOCK, 2 * HEAD_DIM), 1) < HEAD_DIM
            columns = rolled[rows, :]
            for p in range(WIDE // (2 * HEAD_DIM)):
                parts = []
                for h in (2 * p, 2 * p + 1):
                    gap = columns[:, h : h + 1] - flipped[h : h + 1, rows]
                    decay = jnp.exp(jnp.where(causal, gap, -1e30))
                    parts.append((score * decay * flipped[heads + h : heads + h + 1, rows]).astype(BF16))
                lanes = slice(p * 2 * HEAD_DIM, (p + 1) * 2 * HEAD_DIM)
                x = xc_ref[rows, lanes]
                zero = jnp.zeros_like(x)
                both = jnp.concatenate([jnp.where(lower, x, zero), jnp.where(lower, zero, x)], axis=0)
                y = dot(jnp.concatenate(parts, axis=1), both)
                y_ref[rows, lanes] = (y + skip_ref[:, lanes] * x.astype(F32)).astype(BF16)
            return 0

        lax.fori_loop(0, blocks, block, 0)

    @pl.when(i == steps - 1)
    def _():
        log_copy().wait_send()

        def finish(c, _):
            x_copy(c).wait_send()
            b_copy(c).wait_send()
            b_copy(c).wait_recv()
            inc_ref[(1 - side) * per_half + c] = back_in[c]

            @pl.when(pair < pairs - 1)
            def _():
                c_copy(c).wait_send()

            return 0

        lax.fori_loop(0, per_half, finish, 0)


def norm_kernel(
    y_ref, gate_ref, mc_ref, rs_ref, enter_ref, inc_ref, gain_ref, out_ref,
    gated, square, reach, prior,
):
    g, j = pl.program_id(0), pl.program_id(1)
    per_group = pl.num_programs(1)
    groups = pl.num_programs(0)
    length = rs_ref.shape[0]
    heads = rs_ref.shape[1] // 2
    blocks = length // BLOCK

    @pl.when((g == 0) & (j == 0))
    def _():
        total = jnp.zeros((1, heads), F32)
        for b in range(blocks):
            rows = slice(b * BLOCK, (b + 1) * BLOCK)
            running = rs_ref[rows, 0:heads]
            reach[rows] = two_parts(jnp.exp(running))
            prior[b] = jnp.broadcast_to(two_parts(jnp.exp(total)).astype(F32), (8, 2 * heads))
            total = total + running[BLOCK - 1 : BLOCK]

    spread = spread_matrix(g * per_group + j, heads)
    out_maps = mc_ref[...]
    for b in range(blocks):
        rows = slice(b * BLOCK, (b + 1) * BLOCK)
        incoming = inc_ref[0].astype(F32)
        if b > 0:
            keep = dot(prior[b].astype(BF16), spread)[0:1]
            incoming = keep * incoming + enter_ref[b - 1, 0].astype(F32)
        before = dot(out_maps[rows], incoming.astype(BF16))
        value = y_ref[rows].astype(F32) + dot(reach[rows], spread) * before
        value = value * silu(gate_ref[rows].astype(F32))
        gated[j, rows] = value
        part = jnp.sum(value * value, axis=1, keepdims=True)
        part = jnp.broadcast_to(part, (BLOCK, 128))

        @pl.when(j == 0)
        def _():
            square[rows] = part

        @pl.when(j > 0)
        def _():
            square[rows] = square[rows] + part

    @pl.when(j == per_group - 1)
    def _():
        for b in range(blocks):
            rows = slice(b * BLOCK, (b + 1) * BLOCK)
            mean = square[rows][:, 0:1] * (1.0 / (per_group * WIDE))
            inverse = lax.rsqrt(mean + 1e-05)
            for k in range(out_ref.shape[1] // WIDE):
                lanes = slice(k * WIDE, (k + 1) * WIDE)
                out_ref[rows, lanes] = (gated[k, rows] * inverse * gain_ref[:, lanes]).astype(BF16)


def project_kernel(
    tiles, fars, a_ref, w_ref, o_ref, part, send, recv, hop_keep, hop_send, hop_recv,
    s_send, s_recv, h_send, h_recv,
):
    i = pl.program_id(0)
    place = lax.axis_index("tp")
    far, core = place // 2, place % 2
    peer = {"tp": far * 2 + 1 - core}
    share = o_ref.shape[0]

    def across(d):
        return {"tp": (far + d) % fars * 2 + core}

    def near_copy(t):
        return pltpu.make_async_remote_copy(
            send.at[t], recv.at[t], s_send.at[t], s_recv.at[t],
            device_id=peer, device_id_type=MESH,
        )

    def far_copy(t, d):
        at = t * (fars - 1) + d - 1
        return pltpu.make_async_remote_copy(
            hop_send.at[at], hop_recv.at[at], h_send.at[at], h_recv.at[at],
            device_id=across(d), device_id_type=MESH,
        )

    @pl.when(i == 0)
    def _():
        barrier = pltpu.get_barrier_semaphore()
        pl.semaphore_signal(barrier, inc=1, device_id=peer, device_id_type=MESH)
        for d in range(1, fars):
            pl.semaphore_signal(barrier, inc=1, device_id=across(d), device_id_type=MESH)
        pl.semaphore_wait(barrier, fars)

    @pl.when(i < tiles)
    def _():
        part[i % 2] = dot(a_ref[...], w_ref[...])
        for q in range(fars):
            theirs = pl.multiple_of((q * 2 + 1 - core) * share, share)
            send[i, q] = part[i % 2, pl.ds(theirs, share), :].astype(BF16)
        near_copy(i).start()

    @pl.when((i >= 1) & (i < tiles + 1))
    def _():
        t = i - 1
        near_copy(t).wait_recv()
        for d in range(1, fars):
            q = (far + d) % fars
            own = pl.multiple_of((q * 2 + core) * share, share)
            total = part[t % 2, pl.ds(own, share), :] + recv[t, q].astype(F32)
            hop_send[t * (fars - 1) + d - 1] = total.astype(BF16)
            far_copy(t, d).start()
        own = pl.multiple_of((far * 2 + core) * share, share)
        hop_keep[t] = part[t % 2, pl.ds(own, share), :] + recv[t, far].astype(F32)

    @pl.when(i >= 3)
    def _():
        t = i - 3
        total = hop_keep[t]
        for d in range(1, fars):
            far_copy(t, d).wait_recv()
            total = total + hop_recv[t * (fars - 1) + d - 1].astype(F32)
        o_ref[...] = total.astype(BF16)
        near_copy(t).wait_send()
        for d in range(1, fars):
            far_copy(t, d).wait_send()


def whole(shape):
    return pl.BlockSpec(shape, lambda *_: (0,) * len(shape))


def local(
    ctx_size, tp_size, ssm_input, gate_input, state_maps, step_size, decay_rate, skip_gain, conv_weight,
    conv_bias, map_conv, map_bias, norm_gain, out_weight,
):
    length, width = ssm_input.shape
    step_size = jnp.pad(step_size, ((0, 0), (0, HEADS - step_size.shape[1])))
    decay_rate = jnp.pad(decay_rate, (0, HEADS - decay_rate.shape[0]))
    heads = HEADS
    groups = state_maps.shape[2] // STATE
    blocks = length // BLOCK
    chunks = width // WIDE
    per_group = chunks // groups
    maps_width = 2 * groups * STATE
    maps = state_maps.reshape(length, maps_width)
    tail = jnp.concatenate([ssm_input[length - LEAD :], maps[length - LEAD :]], axis=1)
    lead = lax.ppermute(tail, "ctx", [(k, k + 1) for k in range(ctx_size - 1)])
    limit = pltpu.CompilerParams(vmem_limit_bytes=56 * 1024 * 1024)
    shape = jax.ShapeDtypeStruct
    cols = lambda j: (0, j)
    xc, mc, bt, rs, s, enter = pl.pallas_call(
        state_kernel,
        grid=(chunks,),
        in_specs=[
            pl.BlockSpec((length, WIDE), cols),
            pl.BlockSpec((LEAD, WIDE), cols),
            pl.BlockSpec((CONV, WIDE), cols),
            pl.BlockSpec((1, WIDE), cols),
            whole((length, maps_width)),
            pl.BlockSpec((LEAD, maps_width), lambda j: (0, width // maps_width)),
            whole((CONV, maps_width)),
            whole((1, maps_width)),
            whole((length, heads)),
            whole((1, heads)),
        ],
        out_specs=[
            pl.BlockSpec((length, WIDE), cols),
            whole((length, maps_width)),
            whole((groups, STATE, length)),
            whole((length, 2 * heads)),
            pl.BlockSpec((1, STATE, WIDE), lambda j: (j, 0, 0)),
            pl.BlockSpec((blocks - 1, 1, STATE, WIDE), lambda j: (0, j, 0, 0)),
        ],
        out_shape=[
            shape((length, width), BF16),
            shape((length, maps_width), BF16),
            shape((groups, STATE, length), BF16),
            shape((length, 2 * heads), F32),
            shape((chunks, STATE, WIDE), BF16),
            shape((blocks - 1, chunks, STATE, WIDE), BF16),
        ],
        scratch_shapes=[
            pltpu.VMEM((length + LEAD, WIDE), F32),
            pltpu.VMEM((length + LEAD, maps_width), F32),
            pltpu.VMEM((length, 2 * heads), BF16),
            pltpu.VMEM((blocks, 8, 2 * heads), F32),
        ],
        compiler_params=limit,
        name="state",
    )(
        ssm_input, lead, conv_weight, conv_bias[None], maps, lead,
        map_conv.reshape(CONV, maps_width), map_bias.reshape(1, maps_width), step_size,
        decay_rate[None],
    )
    pairs = ctx_size // 2
    per_half = chunks // 2
    steps = max(chunks, per_half + 1 + 2 * (pairs - 1)) + 1
    held = lambda i: (0, jnp.minimum(i, chunks - 1))
    slab = (per_half, STATE, WIDE)
    dma = pltpu.SemaphoreType.DMA
    y, incoming = pl.pallas_call(
        functools.partial(within_kernel, pairs),
        grid=(steps,),
        in_specs=[
            pl.BlockSpec((length, WIDE), held),
            whole((length, maps_width)),
            whole((groups, STATE, length)),
            whole((length, 2 * heads)),
            pl.BlockSpec((1, WIDE), held),
            whole((chunks, STATE, WIDE)),
        ],
        out_specs=[pl.BlockSpec((length, WIDE), held), whole((chunks, STATE, WIDE))],
        out_shape=[shape((length, width), BF16), shape((chunks, STATE, WIDE), BF16)],
        scratch_shapes=[
            pltpu.VMEM((length, 2 * heads), F32),
            pltpu.VMEM((2 * heads, length), F32),
            pltpu.VMEM((8, BLOCK), F32),
            pltpu.VMEM((8, 2 * heads), F32),
            pltpu.VMEM((8, 2 * heads), F32),
            pltpu.VMEM(slab, BF16),
            pltpu.VMEM(slab, BF16),
            pltpu.VMEM(slab, BF16),
            pltpu.VMEM(slab, BF16),
            pltpu.VMEM(slab, BF16),
            dma, dma,
        ] + [dma((per_half,))] * 6,
        compiler_params=pltpu.CompilerParams(
            collective_id=0, has_side_effects=True, vmem_limit_bytes=56 * 1024 * 1024
        ),
        name="within",
    )(xc, mc, bt, rs, jnp.repeat(skip_gain, HEAD_DIM)[None], s)
    at = lambda g, j: (0, g * per_group + j)
    normed = pl.pallas_call(
        norm_kernel,
        grid=(groups, per_group),
        in_specs=[
            pl.BlockSpec((length, WIDE), at),
            pl.BlockSpec((length, WIDE), at),
            pl.BlockSpec((length, STATE), lambda g, j: (0, groups + g)),
            whole((length, 2 * heads)),
            pl.BlockSpec((blocks - 1, 1, STATE, WIDE), lambda g, j: (0, g * per_group + j, 0, 0)),
            pl.BlockSpec((1, STATE, WIDE), lambda g, j: (g * per_group + j, 0, 0)),
            pl.BlockSpec((1, width // groups), lambda g, j: (0, g)),
        ],
        out_specs=pl.BlockSpec((length, width // groups), lambda g, j: (0, g)),
        out_shape=shape((length, width), BF16),
        scratch_shapes=[
            pltpu.VMEM((per_group, length, WIDE), F32),
            pltpu.VMEM((length, 128), F32),
            pltpu.VMEM((length, 2 * heads), BF16),
            pltpu.VMEM((blocks, 8, 2 * heads), F32),
        ],
        compiler_params=limit,
        name="norm",
    )(y, gate_input, mc, rs, enter, incoming, norm_gain[None])
    d_out = out_weight.shape[1]
    tiles = d_out // WIDE
    share = length // tp_size
    fars = tp_size // 2
    hops = tiles * (fars - 1)
    return pl.pallas_call(
        functools.partial(project_kernel, tiles, fars),
        grid=(tiles + 3,),
        in_specs=[
            whole((length, width)),
            pl.BlockSpec((width, WIDE), lambda i: (0, jnp.minimum(i, tiles - 1))),
        ],
        out_specs=pl.BlockSpec((share, WIDE), lambda i: (0, jnp.maximum(i - 3, 0))),
        out_shape=shape((share, d_out), BF16),
        scratch_shapes=[
            pltpu.VMEM((2, length, WIDE), F32),
            pltpu.VMEM((tiles, fars, share, WIDE), BF16),
            pltpu.VMEM((tiles, fars, share, WIDE), BF16),
            pltpu.VMEM((tiles, share, WIDE), F32),
            pltpu.VMEM((hops, share, WIDE), BF16),
            pltpu.VMEM((hops, share, WIDE), BF16),
        ] + [dma((tiles,))] * 2 + [dma((hops,))] * 2,
        compiler_params=pltpu.CompilerParams(
            collective_id=1, has_side_effects=True, vmem_limit_bytes=56 * 1024 * 1024
        ),
        name="project",
    )(normed, out_weight)


def solution(mesh):
    in_specs = (
        P("ctx", "tp"), P("ctx", "tp"), P("ctx", None, "tp"), P("ctx", "tp"), P("tp"), P("tp"),
        P(None, "tp"), P("tp"), P(None, None, "tp"), P(None, "tp"), P("tp"), P("tp", None),
    )
    return jax.shard_map(
        functools.partial(local, mesh.shape["ctx"], mesh.shape["tp"]), mesh=mesh, in_specs=in_specs,
        out_specs=P(("ctx", "tp"), None), check_vma=False,
    )
```

```python
import functools

import jax
import jax.numpy as jnp
from jax import lax
from jax.experimental import pallas as pl
from jax.experimental.pallas import tpu as pltpu
from jax.sharding import PartitionSpec as P

HEAD_DIM = 64
STATE = 128
CONV = 4
BLOCK = 128
WIDE = 512
LEAD = 16
TILE = 256
HEADS = 64
F32 = jnp.float32
BF16 = jnp.bfloat16
MESH = pl.DeviceIdType.MESH


def silu(v):
    half = 0.5 * v
    return half + half * jnp.tanh(half)


def dot(a, b):
    return jnp.dot(a, b, preferred_element_type=F32)


def two_parts(v):
    high = v.astype(BF16)
    low = (v - high.astype(F32)).astype(BF16)
    return jnp.concatenate([high, low], axis=1)


def spread_matrix(chunk, heads):
    rows = lax.broadcasted_iota(jnp.int32, (2 * heads, WIDE), 0)
    cols = lax.broadcasted_iota(jnp.int32, (2 * heads, WIDE), 1)
    rows = jnp.where(rows >= heads, rows - heads, rows)
    return jnp.where(rows == chunk * (WIDE // HEAD_DIM) + cols // HEAD_DIM, 1.0, 0.0).astype(BF16)


def conv_rows(padded, base, count, lanes, weights, bias):
    window = padded[pl.ds(base + LEAD - 8, count + 8), lanes]
    total = bias
    for tap in range(CONV):
        start = 8 - CONV + 1 + tap
        total = total + weights[tap] * window[start : start + count]
    return silu(total)


def mixer_kernel(
    pairs, start, x_ref, x_any, maps_ref, maps_any, cw_ref, cb_ref, mw_ref, mb_ref, step_ref,
    rate_ref, skip_ref, gate_ref, gain_ref, out_ref,
    padded, mpadded, lead_x, lead_m, load, tot, reach, prior, xc, mc, bt, rs, s_all, enter, y_all,
    inc, rolled, flipped, gated, square, mine, theirs, got, chain_in, chain_out, back_out,
    back_in, halo_send, halo_recv, log_send, log_recv, x_send, x_recv, c_send, c_recv, b_send,
    b_recv,
):
    i = pl.program_id(0)
    length = x_ref.shape[0]
    heads = rs.shape[1] // 2
    blocks = length // BLOCK
    groups = bt.shape[0]
    chunks = s_all.shape[0]
    per_half = chunks // 2
    per_group = chunks // groups
    half = 64
    place = lax.axis_index("ctx")
    pair, side = place // 2, place % 2
    first_pair, last_pair = pair == 0, pair == pairs - 1
    final = place == 2 * pairs - 1
    peer = {"ctx": pair * 2 + 1 - side}
    after_me, before_me = {"ctx": place + 1}, {"ctx": place - 1}
    ahead, behind = {"ctx": place + 2}, {"ctx": place - 2}

    def remote(src, dst, send, recv, target):
        return pltpu.make_async_remote_copy(
            src, dst, send, recv, device_id=target, device_id_type=MESH
        )

    def halo_copies():
        rows = pl.ds(length - LEAD, LEAD)
        return (
            remote(x_any.at[rows, :], lead_x, halo_send.at[0], halo_recv.at[0], after_me),
            remote(maps_any.at[rows, :], lead_m, halo_send.at[1], halo_recv.at[1], after_me),
        )

    def log_copy():
        return remote(mine, theirs, log_send, log_recv, peer)

    def x_copy(c):
        src = s_all.at[(1 - side) * per_half + c]
        return remote(src, got.at[c], x_send.at[c], x_recv.at[c], peer)

    def c_copy(c):
        return remote(chain_out.at[c], chain_in.at[c], c_send.at[c], c_recv.at[c], ahead)

    def b_copy(c):
        return remote(back_out.at[c], back_in.at[c], b_send.at[c], b_recv.at[c], peer)

    @pl.when(i == 0)
    def _():
        barrier = pltpu.get_barrier_semaphore()

        def greet(target):
            pl.semaphore_signal(barrier, inc=1, device_id=target, device_id_type=MESH)

        @pl.when(place > 0)
        def _():
            greet(before_me)

        @pl.when(jnp.logical_not(final))
        def _():
            greet(after_me)

        @pl.when(pair > 0)
        def _():
            greet(behind)

        @pl.when(jnp.logical_not(last_pair))
        def _():
            greet(ahead)

        count = (
            jnp.where(place > 0, 1, 0) + jnp.where(final, 0, 1)
            + jnp.where(pair > 0, 1, 0) + jnp.where(last_pair, 0, 1)
        )
        pl.semaphore_wait(barrier, count)

        @pl.when(jnp.logical_not(final))
        def _():
            for copy in halo_copies():
                copy.start()

        tri = (
            lax.broadcasted_iota(jnp.int32, (BLOCK, BLOCK), 0)
            >= lax.broadcasted_iota(jnp.int32, (BLOCK, BLOCK), 1)
        ).astype(F32)
        total = jnp.zeros((1, heads), F32)
        for b in range(blocks):
            rows = slice(b * BLOCK, (b + 1) * BLOCK)
            step = step_ref[:, rows].T
            running = jnp.dot(
                tri, -rate_ref[...] * step,
                precision=lax.Precision.HIGHEST, preferred_element_type=F32,
            )
            rs[rows] = jnp.concatenate([running, step], axis=1)
            last = running[BLOCK - 1 : BLOCK]
            load[rows] = two_parts(jnp.exp(last - running) * step)
            reach[rows] = two_parts(jnp.exp(running))
            tot[b] = jnp.broadcast_to(two_parts(jnp.exp(last)).astype(F32), (8, 2 * heads))
            prior[b] = jnp.broadcast_to(two_parts(jnp.exp(total)).astype(F32), (8, 2 * heads))
            total = total + last
        keep = jnp.exp(total)
        mine[...] = jnp.broadcast_to(jnp.concatenate([keep, keep], axis=1), (8, 2 * heads))
        log_copy().start()
        mpadded[LEAD:] = maps_ref[...].astype(F32)

        @pl.when(place == 0)
        def _():
            lead_x[...] = jnp.zeros_like(lead_x)
            lead_m[...] = jnp.zeros_like(lead_m)

        @pl.when(place > 0)
        def _():
            for copy in halo_copies():
                copy.wait_recv()

        mpadded[0:LEAD] = lead_m[...].astype(F32)
        width = groups * STATE
        for m in range(2):
            lanes = slice(m * width, (m + 1) * width)
            weights = [mw_ref[tap, m : m + 1] for tap in range(CONV)]
            for r in range(length // half):
                mapped = conv_rows(mpadded, r * half, half, lanes, weights, mb_ref[m : m + 1])
                mc[r * half : (r + 1) * half, lanes] = mapped.astype(BF16)
        for b in range(blocks):
            rows = slice(b * BLOCK, (b + 1) * BLOCK)
            for g in range(groups):
                own = mc[rows, g * STATE : (g + 1) * STATE].astype(F32)
                bt[g, :, rows] = own.T.astype(BF16)

    c = (i - 3 - 2 * pair) // 2

    @pl.when((c >= 0) & (c < per_half) & (i >= 3 + 2 * pair) & ((i - 3) % 2 == 0))
    def _():
        @pl.when(c == 0)
        def _():
            log_copy().wait_recv()

        x_copy(c).wait_recv()

        @pl.when(pair > 0)
        def _():
            c_copy(c).wait_recv()

        @pl.when(first_pair)
        def _():
            chain_in[c] = jnp.zeros_like(chain_in[c])

        spread = spread_matrix(side * per_half + c, heads)
        keep_mine = dot(two_parts(mine[:, 0:heads]), spread)[0:1]
        keep_theirs = dot(two_parts(theirs[:, 0:heads]), spread)[0:1]
        own = s_all[side * per_half + c].astype(F32)
        other = got[c].astype(F32)
        early = side == 0
        first = jnp.where(early, own, other)
        second = jnp.where(early, other, own)
        keep_first = jnp.where(early, keep_mine, keep_theirs)
        keep_second = jnp.where(early, keep_theirs, keep_mine)
        before = chain_in[c].astype(F32)
        middle = keep_first * before + first
        after = keep_second * middle + second
        back_out[c] = jnp.where(early, middle, before).astype(BF16)
        b_copy(c).start()

        @pl.when(jnp.logical_not(last_pair))
        def _():
            chain_out[c] = after.astype(BF16)
            c_copy(c).start()

        inc[side * per_half + c] = jnp.where(early, before, middle).astype(BF16)

    @pl.when(i < chunks)
    def _():
        chunk = (i % 2) * per_half + i // 2
        spread = spread_matrix(chunk, heads)
        lanes = pl.ds(pl.multiple_of(chunk * WIDE, WIDE), WIDE)
        padded[0:LEAD] = lead_x[:, lanes].astype(F32)

        def widen(r, _):
            at = pl.multiple_of(r * half, half)
            padded[pl.ds(at + LEAD, half), :] = x_ref[pl.ds(at, half), :].astype(F32)
            return 0

        lax.fori_loop(0, length // half, widen, 0)
        weights, bias = [cw_ref[tap : tap + 1] for tap in range(CONV)], cb_ref[...]

        def conv(r, _):
            at = pl.multiple_of(r * half, half)
            done = conv_rows(padded, at, half, slice(None), weights, bias)
            xc[chunk, pl.ds(at, half), :] = done.astype(BF16)
            return 0

        lax.fori_loop(0, length // half, conv, 0)
        group = chunk // per_group
        state = jnp.zeros((STATE, WIDE), F32)
        for b in range(blocks):
            rows = slice(b * BLOCK, (b + 1) * BLOCK)
            if b > 0:
                enter[b - 1, chunk] = state.astype(BF16)
            scaled = (xc[chunk, rows].astype(F32) * dot(load[rows], spread)).astype(BF16)
            fresh = dot(bt[group, :, rows], scaled)
            if b > 0:
                keep = dot(tot[b].astype(BF16), spread)[0:1]
                state = keep * state + fresh
            else:
                state = fresh
        s_all[chunk] = state.astype(BF16)

        @pl.when(i % 2 == 1)
        def _():
            x_copy(i // 2).start()

    @pl.when((i >= chunks) & (i < 2 * chunks))
    def _():
        chunk = i - chunks
        per = WIDE // HEAD_DIM
        wide = pltpu.roll(rs[...], (2 * heads - chunk * per) % (2 * heads), 1)
        rolled[...] = wide
        turned = wide.T
        flipped[...] = turned[0:per] - jnp.log(turned[heads : heads + per])
        group = chunk // per_group

        def block(b, _):
            at = pl.multiple_of(b * BLOCK, BLOCK)
            rows = pl.ds(at, BLOCK)
            out_map = mc[rows, pl.ds(pl.multiple_of((groups + group) * STATE, STATE), STATE)]
            score = dot(out_map, bt[group, :, rows])
            causal = (
                lax.broadcasted_iota(jnp.int32, (BLOCK, BLOCK), 0)
                >= lax.broadcasted_iota(jnp.int32, (BLOCK, BLOCK), 1)
            )
            score = jnp.where(causal, score, 0.0)
            lower = lax.broadcasted_iota(jnp.int32, (BLOCK, 2 * HEAD_DIM), 1) < HEAD_DIM
            columns = rolled[rows, :]
            for p in range(WIDE // (2 * HEAD_DIM)):
                parts = []
                for h in (2 * p, 2 * p + 1):
                    gap = columns[:, h : h + 1] - flipped[h : h + 1, rows]
                    decay = jnp.exp(jnp.where(causal, gap, -1e30))
                    parts.append((score * decay).astype(BF16))
                lanes = slice(p * 2 * HEAD_DIM, (p + 1) * 2 * HEAD_DIM)
                x = xc[chunk, rows, lanes]
                zero = jnp.zeros_like(x)
                both = jnp.concatenate([jnp.where(lower, x, zero), jnp.where(lower, zero, x)], axis=0)
                y = dot(jnp.concatenate(parts, axis=1), both)
                y_all[chunk, rows, lanes] = (y + skip_ref[:, lanes] * x.astype(F32)).astype(BF16)
            return 0

        lax.fori_loop(0, blocks, block, 0)

    @pl.when(i == start)
    def _():
        log_copy().wait_send()

        @pl.when(jnp.logical_not(final))
        def _():
            for copy in halo_copies():
                copy.wait_send()

        def finish(c, _):
            x_copy(c).wait_send()
            b_copy(c).wait_send()
            b_copy(c).wait_recv()
            inc[(1 - side) * per_half + c] = back_in[c]

            @pl.when(jnp.logical_not(last_pair))
            def _():
                c_copy(c).wait_send()

            return 0

        lax.fori_loop(0, per_half, finish, 0)

    @pl.when(i >= start)
    def _():
        chunk = i - start
        group, j = chunk // per_group, chunk % per_group
        spread = spread_matrix(chunk, heads)
        map_lanes = pl.ds(pl.multiple_of((groups + group) * STATE, STATE), STATE)
        for b in range(blocks):
            rows = slice(b * BLOCK, (b + 1) * BLOCK)
            incoming = inc[chunk].astype(F32)
            if b > 0:
                keep = dot(prior[b].astype(BF16), spread)[0:1]
                incoming = keep * incoming + enter[b - 1, chunk].astype(F32)
            before = dot(mc[rows, map_lanes], incoming.astype(BF16))
            value = y_all[chunk, rows].astype(F32) + dot(reach[rows], spread) * before
            value = value * silu(gate_ref[rows].astype(F32))
            gated[j, rows] = value
            part = jnp.sum(value * value, axis=1, keepdims=True)
            part = jnp.broadcast_to(part, (BLOCK, 128))

            @pl.when(j == 0)
            def _():
                square[rows] = part

            @pl.when(j > 0)
            def _():
                square[rows] = square[rows] + part

        @pl.when(j == per_group - 1)
        def _():
            for b in range(blocks):
                rows = slice(b * BLOCK, (b + 1) * BLOCK)
                mean = square[rows][:, 0:1] * (1.0 / (per_group * WIDE))
                inverse = lax.rsqrt(mean + 1e-05)
                for k in range(out_ref.shape[1] // WIDE):
                    lanes = slice(k * WIDE, (k + 1) * WIDE)
                    scaled = gated[k, rows] * inverse * gain_ref[:, lanes]
                    out_ref[rows, lanes] = scaled.astype(BF16)


def project_kernel(
    tiles, fars, a_ref, w_ref, o_ref, part, send, recv, hop_keep, hop_send, hop_recv,
    s_send, s_recv, h_send, h_recv,
):
    i = pl.program_id(0)
    place = lax.axis_index("tp")
    far, core = place // 2, place % 2
    peer = {"tp": far * 2 + 1 - core}
    share = o_ref.shape[0]

    def across(d):
        return {"tp": (far + d) % fars * 2 + core}

    def near_copy(t):
        return pltpu.make_async_remote_copy(
            send.at[t], recv.at[t], s_send.at[t], s_recv.at[t],
            device_id=peer, device_id_type=MESH,
        )

    def far_copy(t, d):
        at = t * (fars - 1) + d - 1
        return pltpu.make_async_remote_copy(
            hop_send.at[at], hop_recv.at[at], h_send.at[at], h_recv.at[at],
            device_id=across(d), device_id_type=MESH,
        )

    @pl.when(i == 0)
    def _():
        barrier = pltpu.get_barrier_semaphore()
        pl.semaphore_signal(barrier, inc=1, device_id=peer, device_id_type=MESH)
        for d in range(1, fars):
            pl.semaphore_signal(barrier, inc=1, device_id=across(d), device_id_type=MESH)
        pl.semaphore_wait(barrier, fars)

    @pl.when(i < tiles)
    def _():
        part[i % 2] = dot(a_ref[...], w_ref[...])
        for q in range(fars):
            theirs = pl.multiple_of((q * 2 + 1 - core) * share, share)
            send[i, q] = part[i % 2, pl.ds(theirs, share), :].astype(BF16)
        near_copy(i).start()

    @pl.when((i >= 1) & (i < tiles + 1))
    def _():
        t = i - 1
        near_copy(t).wait_recv()
        for d in range(1, fars):
            q = (far + d) % fars
            own = pl.multiple_of((q * 2 + core) * share, share)
            total = part[t % 2, pl.ds(own, share), :] + recv[t, q].astype(F32)
            hop_send[t * (fars - 1) + d - 1] = total.astype(BF16)
            far_copy(t, d).start()
        own = pl.multiple_of((far * 2 + core) * share, share)
        hop_keep[t] = part[t % 2, pl.ds(own, share), :] + recv[t, far].astype(F32)

    @pl.when(i >= 3)
    def _():
        t = i - 3
        total = hop_keep[t]
        for d in range(1, fars):
            far_copy(t, d).wait_recv()
            total = total + hop_recv[t * (fars - 1) + d - 1].astype(F32)
        o_ref[...] = total.astype(BF16)
        near_copy(t).wait_send()
        for d in range(1, fars):
            far_copy(t, d).wait_send()


def whole(shape):
    return pl.BlockSpec(shape, lambda *_: (0,) * len(shape))


def local(
    ctx_size, tp_size, ssm_input, gate_input, state_maps, step_size, decay_rate, skip_gain, conv_weight,
    conv_bias, map_conv, map_bias, norm_gain, out_weight,
):
    length, width = ssm_input.shape
    steps_t = jnp.pad(step_size.T, ((0, HEADS - step_size.shape[1]), (0, 0)))
    decay_rate = jnp.pad(decay_rate, (0, HEADS - decay_rate.shape[0]))
    heads = HEADS
    groups = state_maps.shape[2] // STATE
    blocks = length // BLOCK
    chunks = width // WIDE
    per_half = chunks // 2
    per_group = chunks // groups
    group_width = width // groups
    maps_width = 2 * groups * STATE
    maps = state_maps.reshape(length, maps_width)
    pairs = ctx_size // 2
    start = max(2 * chunks, 2 * (per_half - 1) + 4 + 2 * (pairs - 1))
    shape = jax.ShapeDtypeStruct
    dma = pltpu.SemaphoreType.DMA
    vmem = pltpu.VMEM

    def early(i):
        i = jnp.minimum(i, chunks - 1)
        return (0, (i % 2) * per_half + i // 2)

    def inner(i):
        return (0, jnp.clip(i - chunks, 0, chunks - 1))

    def late(i):
        return (0, jnp.clip(i - start, 0, chunks - 1))

    def late_group(i):
        return (0, jnp.clip(i - start, 0, chunks - 1) // per_group)

    slab = vmem((per_half, STATE, WIDE), BF16)
    normed = pl.pallas_call(
        functools.partial(mixer_kernel, pairs, start),
        grid=(start + chunks,),
        in_specs=[
            pl.BlockSpec((length, WIDE), early),
            pl.BlockSpec(memory_space=pl.ANY),
            whole((length, maps_width)),
            pl.BlockSpec(memory_space=pl.ANY),
            pl.BlockSpec((CONV, WIDE), early),
            pl.BlockSpec((1, WIDE), early),
            whole(map_conv.shape),
            whole(map_bias.shape),
            whole((heads, length)),
            whole((1, heads)),
            pl.BlockSpec((1, WIDE), inner),
            pl.BlockSpec((length, WIDE), late),
            pl.BlockSpec((1, group_width), late_group),
        ],
        out_specs=pl.BlockSpec((length, group_width), late_group),
        out_shape=shape((length, width), BF16),
        scratch_shapes=[
            vmem((length + LEAD, WIDE), F32),
            vmem((length + LEAD, maps_width), F32),
            vmem((LEAD, width), BF16),
            vmem((LEAD, maps_width), BF16),
            vmem((length, 2 * heads), BF16),
            vmem((blocks, 8, 2 * heads), F32),
            vmem((length, 2 * heads), BF16),
            vmem((blocks, 8, 2 * heads), F32),
            vmem((chunks, length, WIDE), BF16),
            vmem((length, maps_width), BF16),
            vmem((groups, STATE, length), BF16),
            vmem((length, 2 * heads), F32),
            vmem((chunks, STATE, WIDE), BF16),
            vmem((blocks - 1, chunks, STATE, WIDE), BF16),
            vmem((chunks, length, WIDE), BF16),
            vmem((chunks, STATE, WIDE), BF16),
            vmem((length, 2 * heads), F32),
            vmem((WIDE // HEAD_DIM, length), F32),
            vmem((per_group, length, WIDE), F32),
            vmem((length, 128), F32),
            vmem((8, 2 * heads), F32),
            vmem((8, 2 * heads), F32),
            slab, slab, slab, slab, slab,
            dma((2,)), dma((2,)), dma, dma,
        ] + [dma((per_half,))] * 6,
        compiler_params=pltpu.CompilerParams(
            collective_id=0, has_side_effects=True, vmem_limit_bytes=56 * 1024 * 1024
        ),
        name="mixer",
    )(
        ssm_input, ssm_input, maps, maps, conv_weight, conv_bias[None], map_conv, map_bias,
        steps_t, decay_rate[None], jnp.repeat(skip_gain, HEAD_DIM)[None], gate_input,
        norm_gain[None],
    )
    d_out = out_weight.shape[1]
    tiles = d_out // TILE
    share = length // tp_size
    fars = tp_size // 2
    hops = tiles * (fars - 1)
    return pl.pallas_call(
        functools.partial(project_kernel, tiles, fars),
        grid=(tiles + 3,),
        in_specs=[
            whole((length, width)),
            pl.BlockSpec((width, TILE), lambda i: (0, jnp.minimum(i, tiles - 1))),
        ],
        out_specs=pl.BlockSpec((share, TILE), lambda i: (0, jnp.maximum(i - 3, 0))),
        out_shape=shape((share, d_out), BF16),
        scratch_shapes=[
            pltpu.VMEM((2, length, TILE), F32),
            pltpu.VMEM((tiles, fars, share, TILE), BF16),
            pltpu.VMEM((tiles, fars, share, TILE), BF16),
            pltpu.VMEM((tiles, share, TILE), F32),
            pltpu.VMEM((hops, share, TILE), BF16),
            pltpu.VMEM((hops, share, TILE), BF16),
        ] + [dma((tiles,))] * 2 + [dma((hops,))] * 2,
        compiler_params=pltpu.CompilerParams(
            collective_id=1, has_side_effects=True, vmem_limit_bytes=56 * 1024 * 1024
        ),
        name="project",
    )(normed, out_weight)


def solution(mesh):
    in_specs = (
        P("ctx", "tp"), P("ctx", "tp"), P("ctx", None, "tp"), P("ctx", "tp"), P("tp"), P("tp"),
        P(None, "tp"), P("tp"), P(None, None, "tp"), P(None, "tp"), P("tp"), P("tp", None),
    )
    return jax.shard_map(
        functools.partial(local, mesh.shape["ctx"], mesh.shape["tp"]), mesh=mesh, in_specs=in_specs,
        out_specs=P(("ctx", "tp"), None), check_vma=False,
    )
```

```python
import functools

import jax
import jax.numpy as jnp
from jax import lax
from jax.experimental import pallas as pl
from jax.experimental.pallas import tpu as pltpu
from jax.sharding import PartitionSpec as P

HEAD_DIM = 64
STATE = 128
CONV = 4
BLOCK = 128
WIDE = 512
LEAD = 16
TILE = 256
NARROW = 256
HEADS = 64
F32 = jnp.float32
BF16 = jnp.bfloat16
MESH = pl.DeviceIdType.MESH


def silu(v):
    half = 0.5 * v
    return half + half * jnp.tanh(half)


def dot(a, b):
    return jnp.dot(a, b, preferred_element_type=F32)


def two_parts(v):
    high = v.astype(BF16)
    low = (v - high.astype(F32)).astype(BF16)
    return jnp.concatenate([high, low], axis=1)


def spread_matrix(chunk, heads):
    rows = lax.broadcasted_iota(jnp.int32, (2 * heads, WIDE), 0)
    cols = lax.broadcasted_iota(jnp.int32, (2 * heads, WIDE), 1)
    rows = jnp.where(rows >= heads, rows - heads, rows)
    return jnp.where(rows == chunk * (WIDE // HEAD_DIM) + cols // HEAD_DIM, 1.0, 0.0).astype(BF16)


def conv_window(window, count, weights, bias):
    total = bias
    for tap in range(CONV):
        start = LEAD - CONV + 1 + tap
        total = total + weights[tap] * window[start : start + count]
    return silu(total)


def conv_rows(padded, base, count, lanes, weights, bias):
    return conv_window(padded[pl.ds(base, count + LEAD), lanes], count, weights, bias)


def mixer_kernel(
    pairs, start, x_ref, x_any, maps_ref, maps_any, cw_ref, cb_ref, mw_ref, mb_ref, step_ref,
    rate_ref, skip_ref, gate_ref, gain_ref, out_ref,
    mpadded, lead_x, lead_m, load, tot, reach, prior, xc, mc, bt, rs, s_all, enter, y_all,
    inc, rolled, flipped, gated, square, mine, theirs, got, chain_in, chain_out, back_out,
    back_in, halo_send, halo_recv, log_send, log_recv, x_send, x_recv, c_send, c_recv, b_send,
    b_recv,
):
    i = pl.program_id(0)
    length = x_ref.shape[0]
    heads = rs.shape[1] // 2
    blocks = length // BLOCK
    groups = bt.shape[0]
    chunks = s_all.shape[0]
    per_half = chunks // 2
    per_group = chunks // groups
    half = 64
    place = lax.axis_index("ctx")
    pair, side = place // 2, place % 2
    first_pair, last_pair = pair == 0, pair == pairs - 1
    final = place == 2 * pairs - 1
    peer = {"ctx": pair * 2 + 1 - side}
    after_me, before_me = {"ctx": place + 1}, {"ctx": place - 1}
    ahead, behind = {"ctx": place + 2}, {"ctx": place - 2}

    def remote(src, dst, send, recv, target):
        return pltpu.make_async_remote_copy(
            src, dst, send, recv, device_id=target, device_id_type=MESH
        )

    def halo_copies():
        rows = pl.ds(length - LEAD, LEAD)
        return (
            remote(x_any.at[rows, :], lead_x, halo_send.at[0], halo_recv.at[0], after_me),
            remote(maps_any.at[rows, :], lead_m, halo_send.at[1], halo_recv.at[1], after_me),
        )

    def log_copy():
        return remote(mine, theirs, log_send, log_recv, peer)

    def x_copy(c):
        src = s_all.at[(1 - side) * per_half + c]
        return remote(src, got.at[c], x_send.at[c], x_recv.at[c], peer)

    def c_copy(c):
        return remote(chain_out.at[c], chain_in.at[c], c_send.at[c], c_recv.at[c], ahead)

    def b_copy(c):
        return remote(back_out.at[c], back_in.at[c], b_send.at[c], b_recv.at[c], peer)

    @pl.when(i == 0)
    def _():
        barrier = pltpu.get_barrier_semaphore()

        def greet(target):
            pl.semaphore_signal(barrier, inc=1, device_id=target, device_id_type=MESH)

        @pl.when(place > 0)
        def _():
            greet(before_me)

        @pl.when(jnp.logical_not(final))
        def _():
            greet(after_me)

        @pl.when(pair > 0)
        def _():
            greet(behind)

        @pl.when(jnp.logical_not(last_pair))
        def _():
            greet(ahead)

        count = (
            jnp.where(place > 0, 1, 0) + jnp.where(final, 0, 1)
            + jnp.where(pair > 0, 1, 0) + jnp.where(last_pair, 0, 1)
        )
        pl.semaphore_wait(barrier, count)

        @pl.when(jnp.logical_not(final))
        def _():
            for copy in halo_copies():
                copy.start()

        tri = (
            lax.broadcasted_iota(jnp.int32, (BLOCK, BLOCK), 0)
            >= lax.broadcasted_iota(jnp.int32, (BLOCK, BLOCK), 1)
        ).astype(F32)
        total = jnp.zeros((1, heads), F32)
        for b in range(blocks):
            rows = slice(b * BLOCK, (b + 1) * BLOCK)
            step = step_ref[:, rows].T
            running = jnp.dot(
                tri, -rate_ref[...] * step,
                precision=lax.Precision.HIGHEST, preferred_element_type=F32,
            )
            rs[rows] = jnp.concatenate([running, step], axis=1)
            last = running[BLOCK - 1 : BLOCK]
            load[rows] = two_parts(jnp.exp(last - running) * step)
            reach[rows] = two_parts(jnp.exp(running))
            tot[b] = jnp.broadcast_to(two_parts(jnp.exp(last)).astype(F32), (8, 2 * heads))
            prior[b] = jnp.broadcast_to(two_parts(jnp.exp(total)).astype(F32), (8, 2 * heads))
            total = total + last
        keep = jnp.exp(total)
        mine[...] = jnp.broadcast_to(jnp.concatenate([keep, keep], axis=1), (8, 2 * heads))
        log_copy().start()
        mpadded[LEAD:] = maps_ref[...].astype(F32)

        @pl.when(place == 0)
        def _():
            lead_x[...] = jnp.zeros_like(lead_x)
            lead_m[...] = jnp.zeros_like(lead_m)

        @pl.when(place > 0)
        def _():
            for copy in halo_copies():
                copy.wait_recv()

        mpadded[0:LEAD] = lead_m[...].astype(F32)
        width = groups * STATE
        for m in range(2):
            lanes = slice(m * width, (m + 1) * width)
            weights = [mw_ref[tap, m : m + 1] for tap in range(CONV)]
            for r in range(length // half):
                mapped = conv_rows(mpadded, r * half, half, lanes, weights, mb_ref[m : m + 1])
                mc[r * half : (r + 1) * half, lanes] = mapped.astype(BF16)
        for b in range(blocks):
            rows = slice(b * BLOCK, (b + 1) * BLOCK)
            for g in range(groups):
                own = mc[rows, g * STATE : (g + 1) * STATE].astype(F32)
                bt[g, :, rows] = own.T.astype(BF16)

    c = (i - 3 - 2 * pair) // 2

    @pl.when((c >= 0) & (c < per_half) & (i >= 3 + 2 * pair) & ((i - 3) % 2 == 0))
    def _():
        @pl.when(c == 0)
        def _():
            log_copy().wait_recv()

        x_copy(c).wait_recv()

        @pl.when(pair > 0)
        def _():
            c_copy(c).wait_recv()

        @pl.when(first_pair)
        def _():
            chain_in[c] = jnp.zeros_like(chain_in[c])

        spread = spread_matrix(side * per_half + c, heads)
        keep_mine = dot(two_parts(mine[:, 0:heads]), spread)[0:1]
        keep_theirs = dot(two_parts(theirs[:, 0:heads]), spread)[0:1]
        own = s_all[side * per_half + c].astype(F32)
        other = got[c].astype(F32)
        early = side == 0
        first = jnp.where(early, own, other)
        second = jnp.where(early, other, own)
        keep_first = jnp.where(early, keep_mine, keep_theirs)
        keep_second = jnp.where(early, keep_theirs, keep_mine)
        before = chain_in[c].astype(F32)
        middle = keep_first * before + first
        after = keep_second * middle + second
        back_out[c] = jnp.where(early, middle, before).astype(BF16)
        b_copy(c).start()

        @pl.when(jnp.logical_not(last_pair))
        def _():
            chain_out[c] = after.astype(BF16)
            c_copy(c).start()

        inc[side * per_half + c] = jnp.where(early, before, middle).astype(BF16)

    @pl.when(i < chunks)
    def _():
        chunk = (i % 2) * per_half + i // 2
        spread = spread_matrix(chunk, heads)
        group = chunk // per_group
        for low in range(0, WIDE, NARROW):
            lanes = slice(low, low + NARROW)
            lead_lanes = pl.ds(pl.multiple_of(chunk * WIDE + low, NARROW), NARROW)
            weights = [cw_ref[tap : tap + 1, lanes] for tap in range(CONV)]
            bias = cb_ref[:, lanes]
            for r in range(length // half):
                at = r * half
                if r == 0:
                    window = jnp.concatenate(
                        [lead_x[:, lead_lanes].astype(F32), x_ref[0:half, lanes].astype(F32)], axis=0
                    )
                else:
                    window = x_ref[at - LEAD : at + half, lanes].astype(F32)
                done = conv_window(window, half, weights, bias)
                xc[chunk, at : at + half, lanes] = done.astype(BF16)
            state = jnp.zeros((STATE, NARROW), F32)
            for b in range(blocks):
                rows = slice(b * BLOCK, (b + 1) * BLOCK)
                if b > 0:
                    enter[b - 1, chunk, :, lanes] = state.astype(BF16)
                factor = dot(load[rows], spread[:, lanes])
                scaled = (xc[chunk, rows, lanes].astype(F32) * factor).astype(BF16)
                fresh = dot(bt[group, :, rows], scaled)
                if b > 0:
                    keep = dot(tot[b].astype(BF16), spread[:, lanes])[0:1]
                    state = keep * state + fresh
                else:
                    state = fresh
            s_all[chunk, :, lanes] = state.astype(BF16)

        @pl.when(i % 2 == 1)
        def _():
            x_copy(i // 2).start()

    @pl.when((i >= chunks) & (i < 2 * chunks))
    def _():
        chunk = i - chunks
        per = WIDE // HEAD_DIM
        wide = pltpu.roll(rs[...], (2 * heads - chunk * per) % (2 * heads), 1)
        rolled[...] = wide
        turned = wide.T
        flipped[...] = turned[0:per] - jnp.log(turned[heads : heads + per])
        group = chunk // per_group

        def block(b, _):
            at = pl.multiple_of(b * BLOCK, BLOCK)
            rows = pl.ds(at, BLOCK)
            out_map = mc[rows, pl.ds(pl.multiple_of((groups + group) * STATE, STATE), STATE)]
            score = dot(out_map, bt[group, :, rows])
            causal = (
                lax.broadcasted_iota(jnp.int32, (BLOCK, BLOCK), 0)
                >= lax.broadcasted_iota(jnp.int32, (BLOCK, BLOCK), 1)
            )
            score = jnp.where(causal, score, 0.0)
            lower = lax.broadcasted_iota(jnp.int32, (BLOCK, 2 * HEAD_DIM), 1) < HEAD_DIM
            columns = rolled[rows, :]
            for p in range(WIDE // (2 * HEAD_DIM)):
                parts = []
                for h in (2 * p, 2 * p + 1):
                    gap = columns[:, h : h + 1] - flipped[h : h + 1, rows]
                    decay = jnp.exp(jnp.where(causal, gap, -1e30))
                    parts.append((score * decay).astype(BF16))
                lanes = slice(p * 2 * HEAD_DIM, (p + 1) * 2 * HEAD_DIM)
                x = xc[chunk, rows, lanes]
                zero = jnp.zeros_like(x)
                both = jnp.concatenate([jnp.where(lower, x, zero), jnp.where(lower, zero, x)], axis=0)
                y = dot(jnp.concatenate(parts, axis=1), both)
                y_all[chunk, rows, lanes] = (y + skip_ref[:, lanes] * x.astype(F32)).astype(BF16)
            return 0

        lax.fori_loop(0, blocks, block, 0, unroll=True)

    @pl.when(i == start)
    def _():
        square[...] = jnp.zeros_like(square)
        log_copy().wait_send()

        @pl.when(jnp.logical_not(final))
        def _():
            for copy in halo_copies():
                copy.wait_send()

        def finish(c, _):
            x_copy(c).wait_send()
            b_copy(c).wait_send()
            b_copy(c).wait_recv()
            inc[(1 - side) * per_half + c] = back_in[c]

            @pl.when(jnp.logical_not(last_pair))
            def _():
                c_copy(c).wait_send()

            return 0

        lax.fori_loop(0, per_half, finish, 0)

    @pl.when(i >= start)
    def _():
        chunk = i - start
        group, j = chunk // per_group, chunk % per_group
        spread = spread_matrix(chunk, heads)
        map_lanes = pl.ds(pl.multiple_of((groups + group) * STATE, STATE), STATE)
        for b in range(blocks):
            rows = slice(b * BLOCK, (b + 1) * BLOCK)
            part = square[rows]
            for low in range(0, WIDE, NARROW):
                lanes = slice(low, low + NARROW)
                incoming = inc[chunk, :, lanes].astype(F32)
                if b > 0:
                    keep = dot(prior[b].astype(BF16), spread[:, lanes])[0:1]
                    incoming = keep * incoming + enter[b - 1, chunk, :, lanes].astype(F32)
                before = dot(mc[rows, map_lanes], incoming.astype(BF16))
                reached = dot(reach[rows], spread[:, lanes])
                value = y_all[chunk, rows, lanes].astype(F32) + reached * before
                value = value * silu(gate_ref[rows, lanes].astype(F32))
                gated[j, rows, lanes] = value
                power = value * value
                for k in range(NARROW // 128):
                    part = part + power[:, k * 128 : (k + 1) * 128]
            square[rows] = part

        @pl.when(j == per_group - 1)
        def _():
            for b in range(blocks):
                rows = slice(b * BLOCK, (b + 1) * BLOCK)
                mean = jnp.sum(square[rows], axis=1, keepdims=True) * (1.0 / (per_group * WIDE))
                inverse = lax.rsqrt(mean + 1e-05)
                for k in range(out_ref.shape[1] // WIDE):
                    lanes = slice(k * WIDE, (k + 1) * WIDE)
                    scaled = gated[k, rows] * inverse * gain_ref[:, lanes]
                    out_ref[rows, lanes] = scaled.astype(BF16)
                square[rows] = jnp.zeros((BLOCK, 128), F32)


def project_kernel(
    tiles, fars, a_ref, w_ref, o_ref, part, send, recv, hop_keep, hop_send, hop_recv,
    s_send, s_recv, h_send, h_recv,
):
    i = pl.program_id(0)
    place = lax.axis_index("tp")
    far, core = place // 2, place % 2
    peer = {"tp": far * 2 + 1 - core}
    share = o_ref.shape[0]

    def across(d):
        return {"tp": (far + d) % fars * 2 + core}

    def near_copy(t):
        return pltpu.make_async_remote_copy(
            send.at[t], recv.at[t], s_send.at[t], s_recv.at[t],
            device_id=peer, device_id_type=MESH,
        )

    def far_copy(t, d):
        at = t * (fars - 1) + d - 1
        return pltpu.make_async_remote_copy(
            hop_send.at[at], hop_recv.at[at], h_send.at[at], h_recv.at[at],
            device_id=across(d), device_id_type=MESH,
        )

    @pl.when(i == 0)
    def _():
        barrier = pltpu.get_barrier_semaphore()
        pl.semaphore_signal(barrier, inc=1, device_id=peer, device_id_type=MESH)
        for d in range(1, fars):
            pl.semaphore_signal(barrier, inc=1, device_id=across(d), device_id_type=MESH)
        pl.semaphore_wait(barrier, fars)

    @pl.when(i < tiles)
    def _():
        part[i % 2] = dot(a_ref[...], w_ref[...])
        for q in range(fars):
            theirs = pl.multiple_of((q * 2 + 1 - core) * share, share)
            send[i, q] = part[i % 2, pl.ds(theirs, share), :].astype(BF16)
        near_copy(i).start()

    @pl.when((i >= 1) & (i < tiles + 1))
    def _():
        t = i - 1
        near_copy(t).wait_recv()
        for d in range(1, fars):
            q = (far + d) % fars
            own = pl.multiple_of((q * 2 + core) * share, share)
            total = part[t % 2, pl.ds(own, share), :] + recv[t, q].astype(F32)
            hop_send[t * (fars - 1) + d - 1] = total.astype(BF16)
            far_copy(t, d).start()
        own = pl.multiple_of((far * 2 + core) * share, share)
        hop_keep[t] = part[t % 2, pl.ds(own, share), :] + recv[t, far].astype(F32)

    @pl.when(i >= 3)
    def _():
        t = i - 3
        total = hop_keep[t]
        for d in range(1, fars):
            far_copy(t, d).wait_recv()
            total = total + hop_recv[t * (fars - 1) + d - 1].astype(F32)
        o_ref[...] = total.astype(BF16)
        near_copy(t).wait_send()
        for d in range(1, fars):
            far_copy(t, d).wait_send()


def whole(shape):
    return pl.BlockSpec(shape, lambda *_: (0,) * len(shape))


def local(
    ctx_size, tp_size, ssm_input, gate_input, state_maps, step_size, decay_rate, skip_gain, conv_weight,
    conv_bias, map_conv, map_bias, norm_gain, out_weight,
):
    length, width = ssm_input.shape
    steps_t = jnp.pad(step_size.T, ((0, HEADS - step_size.shape[1]), (0, 0)))
    decay_rate = jnp.pad(decay_rate, (0, HEADS - decay_rate.shape[0]))
    heads = HEADS
    groups = state_maps.shape[2] // STATE
    blocks = length // BLOCK
    chunks = width // WIDE
    per_half = chunks // 2
    per_group = chunks // groups
    group_width = width // groups
    maps_width = 2 * groups * STATE
    maps = state_maps.reshape(length, maps_width)
    pairs = ctx_size // 2
    start = max(2 * chunks, 2 * (per_half - 1) + 4 + 2 * (pairs - 1))
    shape = jax.ShapeDtypeStruct
    dma = pltpu.SemaphoreType.DMA
    vmem = pltpu.VMEM

    def early(i):
        i = jnp.minimum(i, chunks - 1)
        return (0, (i % 2) * per_half + i // 2)

    def inner(i):
        return (0, jnp.clip(i - chunks, 0, chunks - 1))

    def late(i):
        return (0, jnp.clip(i - start, 0, chunks - 1))

    def late_group(i):
        return (0, jnp.clip(i - start, 0, chunks - 1) // per_group)

    slab = vmem((per_half, STATE, WIDE), BF16)
    normed = pl.pallas_call(
        functools.partial(mixer_kernel, pairs, start),
        grid=(start + chunks,),
        in_specs=[
            pl.BlockSpec((length, WIDE), early),
            pl.BlockSpec(memory_space=pl.ANY),
            whole((length, maps_width)),
            pl.BlockSpec(memory_space=pl.ANY),
            pl.BlockSpec((CONV, WIDE), early),
            pl.BlockSpec((1, WIDE), early),
            whole(map_conv.shape),
            whole(map_bias.shape),
            whole((heads, length)),
            whole((1, heads)),
            pl.BlockSpec((1, WIDE), inner),
            pl.BlockSpec((length, WIDE), late),
            pl.BlockSpec((1, group_width), late_group),
        ],
        out_specs=pl.BlockSpec((length, group_width), late_group),
        out_shape=shape((length, width), BF16),
        scratch_shapes=[
            vmem((length + LEAD, maps_width), F32),
            vmem((LEAD, width), BF16),
            vmem((LEAD, maps_width), BF16),
            vmem((length, 2 * heads), BF16),
            vmem((blocks, 8, 2 * heads), F32),
            vmem((length, 2 * heads), BF16),
            vmem((blocks, 8, 2 * heads), F32),
            vmem((chunks, length, WIDE), BF16),
            vmem((length, maps_width), BF16),
            vmem((groups, STATE, length), BF16),
            vmem((length, 2 * heads), F32),
            vmem((chunks, STATE, WIDE), BF16),
            vmem((blocks - 1, chunks, STATE, WIDE), BF16),
            vmem((chunks, length, WIDE), BF16),
            vmem((chunks, STATE, WIDE), BF16),
            vmem((length, 2 * heads), F32),
            vmem((WIDE // HEAD_DIM, length), F32),
            vmem((per_group, length, WIDE), F32),
            vmem((length, 128), F32),
            vmem((8, 2 * heads), F32),
            vmem((8, 2 * heads), F32),
            slab, slab, slab, slab, slab,
            dma((2,)), dma((2,)), dma, dma,
        ] + [dma((per_half,))] * 6,
        compiler_params=pltpu.CompilerParams(
            collective_id=0, has_side_effects=True, vmem_limit_bytes=56 * 1024 * 1024
        ),
        name="mixer",
    )(
        ssm_input, ssm_input, maps, maps, conv_weight, conv_bias[None], map_conv, map_bias,
        steps_t, decay_rate[None], jnp.repeat(skip_gain, HEAD_DIM)[None], gate_input,
        norm_gain[None],
    )
    d_out = out_weight.shape[1]
    tiles = d_out // TILE
    share = length // tp_size
    fars = tp_size // 2
    hops = tiles * (fars - 1)
    return pl.pallas_call(
        functools.partial(project_kernel, tiles, fars),
        grid=(tiles + 3,),
        in_specs=[
            whole((length, width)),
            pl.BlockSpec((width, TILE), lambda i: (0, jnp.minimum(i, tiles - 1))),
        ],
        out_specs=pl.BlockSpec((share, TILE), lambda i: (0, jnp.maximum(i - 3, 0))),
        out_shape=shape((share, d_out), BF16),
        scratch_shapes=[
            pltpu.VMEM((2, length, TILE), F32),
            pltpu.VMEM((tiles, fars, share, TILE), BF16),
            pltpu.VMEM((tiles, fars, share, TILE), BF16),
            pltpu.VMEM((tiles, share, TILE), F32),
            pltpu.VMEM((hops, share, TILE), BF16),
            pltpu.VMEM((hops, share, TILE), BF16),
        ] + [dma((tiles,))] * 2 + [dma((hops,))] * 2,
        compiler_params=pltpu.CompilerParams(
            collective_id=1, has_side_effects=True, vmem_limit_bytes=56 * 1024 * 1024
        ),
        name="project",
    )(normed, out_weight)


def solution(mesh):
    in_specs = (
        P("ctx", "tp"), P("ctx", "tp"), P("ctx", None, "tp"), P("ctx", "tp"), P("tp"), P("tp"),
        P(None, "tp"), P("tp"), P(None, None, "tp"), P(None, "tp"), P("tp"), P("tp", None),
    )
    return jax.shard_map(
        functools.partial(local, mesh.shape["ctx"], mesh.shape["tp"]), mesh=mesh, in_specs=in_specs,
        out_specs=P(("ctx", "tp"), None), check_vma=False,
    )
```
